256 devices in a mesh: row: 4 (over x), col: 16 (over y, z_lo), sample: 4 (over z_hi, core).
Axes of the slice: x: 4, y: 4, z: 8 (z_hi: 2, z_lo: 4; z = z_hi * 4 + z_lo), core: 2. Of those that a mesh axis runs over, the one named last changes fastest.
Arguments:
- pair: bfloat16 [2048, 2048, 128], P('row', ('col', 'sample')), may hold values from -6 to 6
- pair_gain: float32 [128], replicated, may hold values from 0.25 to 1.75
- pair_weight: bfloat16 [128, 16], replicated, may hold values from -0.5 to 0.5
- queries: bfloat16 [40, 16, 48, 2048], P('sample', 'col', None, 'row'), may hold values from -400 to 400
- keys: bfloat16 [40, 16, 48, 2048], P('sample', 'col', None, 'row'), may hold values from -5 to 5
- values: bfloat16 [40, 16, 48, 2048], P('sample', 'col', None, 'row'), may hold values from -6 to 6
- d_atoms: bfloat16 [40, 16, 48, 8192], P('sample', 'col', None, 'row'), may hold values from -768 to 768
- key_mask: int32 [2048], P('row'), may hold values 0 or 1
- atom_token: int32 [8192], P('row'), may hold values from 0 to 2047, as said below
Outputs:
- attn_out: bfloat16 [40, 16, 48, 2048], P('sample', 'col', None, 'row')
- d_query: bfloat16 [40, 16, 48, 2048], P('sample', 'col', None, 'row')
- d_pair: bfloat16 [2048, 2048, 128], P('row', ('col', 'sample'))
The draws below stay inside these ranges and needn't reach their ends.
Inputs may be any that keep to these rules, and one draw needn't show every extreme that they name: `atom_token`: the atoms of the i-th aligned block of 2048 atoms name tokens of the i-th block of 512 tokens, the block's first and last token among them.
All inputs are finite; a program needn't handle non-finite values. No bound on the sum of `key_mask` on one device may be relied on, other than what follows from the above.
Results may differ from the reference program's by a relative error of at most 0.025.
Values may be sent and summed in bfloat16 or wider, within the bound.
No kernel may reach another device: no remote copies, remote signals or barrier semaphores. Data moves between devices by JAX's collectives and lax.ppermute only.
A program may use at most 128 MiB of HBM per device.

```python
import math
import jax
import jax.numpy as jnp
from jax import lax

C = 128
H = 16
DH = 48
STRIP = 512
TOKENS = 2048
SAMPLES = 40
ATOMS = 8192


def key_base(key):
    return jnp.clip(jax.random.normal(key, (SAMPLES, H, DH, TOKENS), jnp.float32), -5.0, 5.0)


def draw_keys(key, part):
    base = key_base(key)
    return base.astype(jnp.bfloat16)


def draw_queries(key, part):
    base = key_base(key)
    key = jax.random.fold_in(key, 7)
    return jax.random.normal(key, base.shape, jnp.float32).astype(jnp.bfloat16)


def draw_atom_token(key, part):
    key = jax.random.fold_in(key, 5)
    per_strip = 4 * STRIP
    local = jax.random.randint(key, (ATOMS,), 0, STRIP)
    position = jnp.arange(ATOMS) % per_strip
    local = jnp.where(position == 0, 0, jnp.where(position == per_strip - 1, STRIP - 1, local))
    return (jnp.arange(ATOMS) // per_strip * STRIP + local).astype(jnp.int32)


def touch_ends(drawn, rng, low, top_value):
    dims = drawn.shape
    index_at = [jax.random.randint(jax.random.fold_in(rng, axis), (), 0, dims[axis]) for axis in range(len(dims))]
    drawn = drawn.at[tuple(index_at)].set(low)
    longest = dims.index(max(dims))
    index_at[longest] = (index_at[longest] + 1) % dims[longest]
    return drawn.at[tuple(index_at)].set(top_value)


def levels(stream_key, shape, split, smallest, top_value):
    def one(dim, blocks):
        heights = jax.random.uniform(jax.random.fold_in(jax.random.fold_in(stream_key, 6), dim), (blocks,), jnp.float32, smallest / len(split), top_value / len(split))
        return jnp.repeat(jnp.exp(heights), shape[dim] // blocks).reshape((-1,) + (1,) * (len(shape) - dim - 1))

    loudness = one(*split[0])
    for cut in split[1:]:
        loudness = loudness * one(*cut)
    return loudness


def gaussian(stream_key, dims, spread, bound, split=(), kind=jnp.bfloat16):
    factor_of = levels(stream_key, dims, split, -0.22, 0.18) if split else 1.0
    array = jax.random.normal(stream_key, dims, jnp.float32) * spread * factor_of
    return jnp.minimum(jnp.maximum(array, -bound), bound).astype(kind)


def setup_inputs(seed: int = 0) -> dict:
    arg_keys = jax.random.split(jax.random.key(seed), 10)
    return {
        "pair": gaussian(arg_keys[0], (TOKENS, TOKENS, C), 1.0, 6.0, ((0, 4), (1, 64))),
        "pair_gain": jnp.clip(1.0 + 0.15 * jax.random.normal(arg_keys[1], (C,), jnp.float32), 0.25, 1.75),
        "pair_weight": gaussian(arg_keys[2], (C, H), C ** -0.5, 0.5),
        "queries": draw_queries(jax.random.fold_in(arg_keys[9], 71), 0),
        "keys": draw_keys(jax.random.fold_in(arg_keys[9], 71), 0),
        "values": gaussian(arg_keys[5], (SAMPLES, H, DH, TOKENS), 1.0, 6.0, ((0, 4), (1, 16), (3, 4))),
        "d_atoms": gaussian(arg_keys[6], (SAMPLES, H, DH, ATOMS), (TOKENS // 16), 768.0, ((0, 4), (1, 16), (3, 4))),
        "key_mask": touch_ends((jax.random.randint(arg_keys[7], (TOKENS,), 0, 16) < 15).astype(jnp.int32), jax.random.fold_in(arg_keys[7], 1), 0, 1),
        "atom_token": draw_atom_token(jax.random.fold_in(arg_keys[9], 71), 0),
    }


EPS = 1e-05
HIGH = lax.Precision.HIGHEST

def normalize(pair_block, pair_gain):
    widened = pair_block.astype(jnp.float32)
    centred = widened - lax.optimization_barrier(jnp.mean(widened, axis=-1, keepdims=True))
    inverse = lax.rsqrt(lax.optimization_barrier(jnp.mean(centred * centred, axis=-1, keepdims=True)) + EPS)
    hatted = centred * inverse
    return ((hatted * pair_gain).astype(jnp.bfloat16), hatted, inverse)

def norm_backward(d_normed, hatted, inverse, pair_gain):
    scaled = d_normed * pair_gain
    return inverse * (scaled - lax.optimization_barrier(jnp.mean(scaled, axis=-1, keepdims=True)) - hatted * lax.optimization_barrier(jnp.mean(scaled * hatted, axis=-1, keepdims=True)))

def reference(pair, pair_gain, pair_weight, queries, keys, values, d_atoms, key_mask, atom_token):
    count_all = pair.shape[0]
    channels = pair.shape[2]
    block_rows = math.gcd(count_all, 128)
    block_count = count_all // block_rows
    scaling = 1.0 / math.sqrt(DH)
    block_ids = jnp.arange(block_count, dtype=jnp.int32)

    def project(block_index):
        pair_block = lax.dynamic_slice_in_dim(pair, block_index * block_rows, block_rows, 0)
        normed = normalize(pair_block, pair_gain)[0]
        projected = jnp.dot(normed.reshape(-1, channels), pair_weight, preferred_element_type=jnp.float32)
        return projected.astype(jnp.bfloat16).reshape(block_rows, count_all, H)
    bias_rows = lax.map(project, block_ids).reshape(count_all, count_all, H)
    bias_heads = jnp.transpose(bias_rows, (2, 0, 1))
    usable = key_mask > 0

    def per_head(head):
        head_bias = bias_heads[head].astype(jnp.float32)
        atom_terms = jnp.moveaxis(d_atoms[:, head], 2, 0).astype(jnp.float32)
        summed = jax.ops.segment_sum(atom_terms, atom_token, num_segments=count_all)
        grad_out = jnp.moveaxis(summed, 0, 2).astype(jnp.bfloat16)

        def per_sample(running, inputs):
            query_cols, key_cols, value_cols, grad_cols = inputs
            scores = jnp.dot(query_cols.T, key_cols, preferred_element_type=jnp.float32) * scaling + head_bias
            scores = jnp.where(usable[None, :], scores, -1000000000.0)
            exponent = jnp.exp(scores - lax.optimization_barrier(jnp.max(scores, axis=1, keepdims=True)))
            chances = exponent / lax.optimization_barrier(jnp.sum(exponent, axis=1, keepdims=True))
            weights = chances.astype(jnp.bfloat16)
            output = jnp.dot(weights, value_cols.T, preferred_element_type=jnp.float32).T.astype(jnp.bfloat16)
            d_chances = jnp.dot(grad_cols.T, value_cols, preferred_element_type=jnp.float32)
            centre = lax.optimization_barrier(jnp.sum(grad_cols.astype(jnp.float32) * output.astype(jnp.float32), axis=0))
            d_scores = chances * (d_chances - centre[:, None])
            d_weights = d_scores.astype(jnp.bfloat16)
            d_query = (jnp.dot(d_weights, key_cols.T, preferred_element_type=jnp.float32) * scaling).T.astype(jnp.bfloat16)
            return (running + d_scores, (output, d_query))
        zeros_start = jnp.zeros((count_all, count_all), jnp.float32)
        d_bias_head, (outputs, d_queries) = lax.scan(per_sample, zeros_start, (queries[:, head], keys[:, head], values[:, head], grad_out))
        return (outputs, d_queries, d_bias_head)
    outputs, d_queries, d_bias = lax.map(per_head, jnp.arange(H, dtype=jnp.int32))

    def pair_grad(block_index):
        pair_block = lax.dynamic_slice_in_dim(pair, block_index * block_rows, block_rows, 0)
        normed, hatted, inverse = normalize(pair_block, pair_gain)
        grad_block = lax.dynamic_slice_in_dim(d_bias, block_index * block_rows, block_rows, 1)
        d_normed = jnp.einsum('hqk,ch->qkc', grad_block, pair_weight.astype(jnp.float32), precision=HIGH)
        return norm_backward(d_normed, hatted, inverse, pair_gain).astype(jnp.bfloat16)
    d_pair = lax.map(pair_grad, block_ids).reshape(count_all, count_all, channels)
    return (jnp.swapaxes(outputs, 0, 1), jnp.swapaxes(d_queries, 0, 1), d_pair)
```

```python
import functools
import math

import jax
import jax.numpy as jnp
from jax import lax
from jax.experimental import pallas as pl
from jax.experimental.pallas import tpu as pltpu
from jax.sharding import Mesh, PartitionSpec as P

EPS = 1e-05
HIGH = lax.Precision.HIGHEST
F32, BF16 = jnp.float32, jnp.bfloat16
LOG2E = 1.4426950408889634
NEG = -1e9
TN = (((0,), (0,)), ((), ()))


def attn_kernel(JT, core_ref, mine_ref, other_ref, q_ref, k_ref, v_ref, m_ref, g_ref,
                o_ref, dq_ref, keep_ref, send_ref,
                bias_s, acc_s, s_s, e_s, kt_s, vt_s, kc_s, vc_s):
    step = pl.program_id(0)
    steps = pl.num_programs(0)
    n_i = q_ref.shape[-1]
    dh = q_ref.shape[-2]
    n_j = bias_s.shape[0]
    rows = k_ref.shape[0]
    per = n_j // rows
    core = core_ref[0]
    blocks = mine_ref.shape[0]
    bj = mine_ref.shape[1]
    scaling = 1.0 / math.sqrt(dh)

    @pl.when(step == 0)
    def _():
        for src, par in ((mine_ref, core), (other_ref, 1 - core)):
            @pl.loop(0, blocks)
            def _(b):
                at = pl.multiple_of((b * 2 + par) * bj, bj)
                bias_s[pl.ds(at, bj), :] = src[b].astype(F32) * LOG2E
        mcol = jnp.concatenate([m_ref[r, 0, :8, :].astype(F32) for r in range(rows)], 1).T
        for t in range(0, n_j, 256):
            m = mcol[t:t + 256, 0:1]
            bias_s[t:t + 256, :] = jnp.where(m > 0, bias_s[t:t + 256, :], NEG)
        acc_s[...] = jnp.zeros_like(acc_s)


    for r in range(rows):
        sl = slice(r * per, (r + 1) * per)
        k = k_ref[r, 0]
        v = v_ref[r, 0]
        kz = k * m_ref[r, 0]
        kt_s[sl, :] = jnp.concatenate([kz, kz], 0).T
        one = jnp.ones((16, per), BF16)
        vt_s[sl, :] = jnp.concatenate([v, v, one], 0).T
        kc_s[:, sl] = k
        vc_s[:, sl] = jnp.concatenate([v, one], 0)

    q = q_ref[0].astype(F32) * (scaling * LOG2E)
    qh = q.astype(BF16)
    ql = (q - qh.astype(F32)).astype(BF16)
    q2 = jnp.concatenate([qh, ql], 0)
    IH = 256
    for h in range(n_i // IH):
        il = slice(h * IH, (h + 1) * IH)
        m = None
        for t in range(0, n_j, JT):
            s = jnp.dot(kt_s[t:t + JT, :], q2[:, il], preferred_element_type=F32) + bias_s[t:t + JT, il]
            s_s[t:t + JT, :] = s
            mt = jnp.max(s.reshape(JT // 8, 8, IH), axis=0)
            m = mt if m is None else jnp.maximum(m, mt)
        m = jnp.max(m, axis=0, keepdims=True)
        o = None
        for t in range(0, n_j, JT):
            e = jnp.exp2(s_s[t:t + JT, :] - m).astype(BF16)
            e_s[t:t + JT, :] = e
            ot = jnp.dot(vc_s[:, t:t + JT], e, preferred_element_type=F32)
            o = ot if o is None else o + ot
        inv = 1.0 / o[dh:dh + 1, :]
        o = o[:dh] * inv
        o_ref[0, :, il] = o.astype(BF16)
        g = g_ref[0, :, il].astype(F32)
        centre = jnp.sum(g * o, axis=0, keepdims=True)
        g = g * inv
        c = -centre * inv
        gh = g.astype(BF16)
        gl = (g - gh.astype(F32)).astype(BF16)
        ch = c.astype(BF16).astype(F32)
        cl = c - ch
        row = lax.broadcasted_iota(jnp.int32, (16, IH), 0)
        cb = jnp.where(row == 0, ch, jnp.where(row == 1, cl, 0.0)).astype(BF16)
        g2 = jnp.concatenate([gh, gl, cb], 0)
        dq = None
        for t in range(0, n_j, JT):
            x = jnp.dot(vt_s[t:t + JT, :], g2, preferred_element_type=F32)
            ds = e_s[t:t + JT, :].astype(F32) * x
            acc_s[t:t + JT, il] += ds
            dt = jnp.dot(kc_s[:, t:t + JT], ds.astype(BF16), preferred_element_type=F32)
            dq = dt if dq is None else dq + dt
        dq_ref[0, :, il] = (dq * scaling).astype(BF16)

    @pl.when(step == steps - 1)
    def _():
        for dst, par in ((keep_ref, core), (send_ref, 1 - core)):
            @pl.loop(0, blocks)
            def _(b):
                at = pl.multiple_of((b * 2 + par) * bj, bj)
                dst[b] = acc_s[pl.ds(at, bj), :].astype(BF16)


def attention(core, mine, other, q, kv, g, JT=1024):
    S, dh, I = q.shape
    R, per = kv.shape[0], kv.shape[3]
    J = R * per
    full = lambda a: pl.BlockSpec(a.shape, lambda s: (0,) * a.ndim)
    qspec = pl.BlockSpec((1, dh, I), lambda s: (s, 0, 0))
    kspec = pl.BlockSpec((R, 1, dh, per), lambda s: (0, s, 0, 0))
    vspec = pl.BlockSpec((R, 1, dh, per), lambda s: (0, s + S, 0, 0))
    mspec = pl.BlockSpec((R, 1, dh, per), lambda s: (0, 2 * S, 0, 0))
    IH = 256
    return pl.pallas_call(
        functools.partial(attn_kernel, JT),
        grid=(S,),
        in_specs=[pl.BlockSpec(memory_space=pltpu.SMEM), full(mine), full(other),
                  qspec, kspec, vspec, mspec, qspec],
        out_specs=[qspec, qspec, full(mine), full(other)],
        out_shape=[jax.ShapeDtypeStruct(q.shape, BF16), jax.ShapeDtypeStruct(q.shape, BF16),
                   jax.ShapeDtypeStruct(mine.shape, BF16), jax.ShapeDtypeStruct(other.shape, BF16)],
        scratch_shapes=[pltpu.VMEM((J, I), F32), pltpu.VMEM((J, I), F32),
                        pltpu.VMEM((J, IH), F32), pltpu.VMEM((J, IH), BF16),
                        pltpu.VMEM((J, 2 * dh), BF16), pltpu.VMEM((J, 2 * dh + 16), BF16),
                        pltpu.VMEM((dh, J), BF16), pltpu.VMEM((dh + 16, J), BF16)],
        compiler_params=pltpu.CompilerParams(vmem_limit_bytes=48 * 1024 * 1024),
        cost_estimate=pl.CostEstimate(flops=8 * S * J * I * dh, bytes_accessed=12 * 1024 * 1024, transcendentals=S * I * J),
        name="attend",
    )(core, mine, other, q, kv, kv, kv, g)


def normalize(pair_block, pair_gain):
    widened = pair_block.astype(F32)
    centred = widened - jnp.mean(widened, axis=-1, keepdims=True)
    inverse = lax.rsqrt(jnp.mean(centred * centred, axis=-1, keepdims=True) + EPS)
    hatted = centred * inverse
    return ((hatted * pair_gain).astype(BF16), hatted, inverse)


def norm_backward(d_normed, hatted, inverse, pair_gain):
    scaled = d_normed * pair_gain
    return inverse * (
        scaled
        - jnp.mean(scaled, axis=-1, keepdims=True)
        - hatted * jnp.mean(scaled * hatted, axis=-1, keepdims=True)
    )


def local(pair, pair_gain, pair_weight, queries, keys, values, d_atoms, key_mask, atom_token):
    samples, _, dh, strip = queries.shape
    flags = jnp.broadcast_to(key_mask.astype(BF16), (1, dh, strip))
    kv = lax.all_gather(jnp.concatenate([keys[:, 0], values[:, 0], flags], 0), "row")

    normed, hatted, inverse = normalize(pair, pair_gain)
    tile_bias = jnp.einsum(
        "rwc,ch->hwr", normed, pair_weight, preferred_element_type=F32
    ).astype(BF16)
    heads, width, _ = tile_bias.shape
    out = jnp.broadcast_to(tile_bias[:, None], (heads, 2, width, strip)).reshape(2 * heads, width, strip)
    mine = lax.all_to_all(out, ("col", "zhi"), 0, 0, tiled=True)
    other = lax.ppermute(mine, "core", [(0, 1), (1, 0)])

    offset = lax.axis_index("row") * strip
    onehot = (
        atom_token[:, None] - offset == jnp.arange(strip, dtype=jnp.int32)[None, :]
    ).astype(BF16)
    grad_out = jnp.einsum(
        "sda,at->sdt", d_atoms[:, 0], onehot, preferred_element_type=F32
    ).astype(BF16)

    core = lax.axis_index("core").astype(jnp.int32).reshape(1)
    o, dq, keep, send = attention(core, mine, other, queries[:, 0], kv, grad_out)

    got = lax.ppermute(send, "core", [(0, 1), (1, 0)])
    chip = (keep.astype(F32) + got.astype(F32)).astype(BF16)
    parts = lax.all_to_all(chip, ("col", "zhi"), 0, 0, tiled=True)
    tile_grad = jnp.sum(parts.reshape(heads, 2, width, strip).astype(F32), axis=1)
    d_normed = jnp.einsum("hwr,ch->rwc", tile_grad, pair_weight.astype(F32), precision=HIGH)
    d_pair = norm_backward(d_normed, hatted, inverse, pair_gain).astype(BF16)
    return (o[:, None], dq[:, None], d_pair)


def solution(mesh):
    fine = Mesh(mesh.devices.reshape(4, 16, 2, 2), ("row", "col", "zhi", "core"))
    sample = ("zhi", "core")
    tokens = P(sample, "col", None, "row")
    tile = P("row", ("col", "zhi", "core"), None)
    return jax.shard_map(
        local,
        mesh=fine,
        in_specs=(tile, P(), P(), tokens, tokens, tokens, tokens, P("row"), P("row")),
        out_specs=(tokens, tokens, tile),
        check_vma=False,
    )
```

```python
import math

import jax
import jax.numpy as jnp
from jax import lax
from jax.experimental import pallas as pl
from jax.experimental.pallas import tpu as pltpu
from jax.sharding import Mesh, PartitionSpec as P

F32, BF16 = jnp.float32, jnp.bfloat16
EPS = 1e-05
LOG2E = 1.4426950408889634
NEG = -1e9
GROUP = 8


def split(x):
    hi = x.astype(BF16)
    return hi, (x - hi.astype(F32)).astype(BF16)


def spread(w):
    rows, c = w.shape
    tall = jnp.broadcast_to(w[:, None, :], (rows, GROUP, c)).reshape(rows * GROUP, c)
    line = lax.broadcasted_iota(jnp.int32, tall.shape, 0) % GROUP
    return jnp.concatenate([jnp.where(line == j, tall, 0.0) for j in range(GROUP)], 1)


def bias_kernel(pair_ref, gain_ref, weight_ref, out_ref, hat_ref, inv_ref, x_s):
    rows, width, chan = pair_ref.shape
    heads, copies = out_ref.shape[:2]
    pitch = width + 1
    for i in range(rows):
        x_s[i * pitch:i * pitch + width, :] = pair_ref[i].astype(F32)
    gain = jnp.broadcast_to(gain_ref[...], (GROUP, chan)).T[:, 0:1]
    weight = spread(weight_ref[...].astype(F32)).astype(BF16)
    found = []
    for g in range(width // GROUP):
        cols = []
        for j in range(g * GROUP, (g + 1) * GROUP):
            x = x_s[pl.ds(j, rows, stride=pitch), :].astype(BF16).T.astype(F32)
            cen = x - jnp.mean(x, axis=0, keepdims=True)
            inv = lax.rsqrt(jnp.mean(cen * cen, axis=0, keepdims=True) + EPS)
            hat = cen * inv
            inv_ref[j:j + 1, :] = inv
            hat_ref[j] = hat.astype(BF16)
            cols.append((hat * gain).astype(BF16))
        tile = jnp.dot(weight, jnp.concatenate(cols, 0), preferred_element_type=F32)
        found.append(tile.reshape(heads, GROUP, rows))
    for g in range(0, width // GROUP, 2):
        both = jnp.concatenate(found[g:g + 2], 1).astype(BF16)
        for z in range(copies):
            out_ref[:, z, g * GROUP:(g + 2) * GROUP, :] = both


def pair_bias(pair, gain, weight, copies, block=256):
    I, W, C = pair.shape
    H = weight.shape[1]
    return pl.pallas_call(
        bias_kernel,
        grid=(I // block,),
        in_specs=[pl.BlockSpec((block, W, C), lambda n: (n, 0, 0)),
                  pl.BlockSpec((1, C), lambda n: (0, 0)),
                  pl.BlockSpec((H, C), lambda n: (0, 0))],
        out_specs=[pl.BlockSpec((H, copies, W, block), lambda n: (0, 0, 0, n)),
                   pl.BlockSpec((W, C, block), lambda n: (0, 0, n)),
                   pl.BlockSpec((W, block), lambda n: (0, n))],
        out_shape=[jax.ShapeDtypeStruct((H, copies, W, I), BF16),
                   jax.ShapeDtypeStruct((W, C, I), BF16),
                   jax.ShapeDtypeStruct((W, I), F32)],
        scratch_shapes=[pltpu.VMEM((block * (W + 1), C), F32)],
        compiler_params=pltpu.CompilerParams(vmem_limit_bytes=32 * 1024 * 1024),
        cost_estimate=pl.CostEstimate(flops=20 << 30, bytes_accessed=40 << 20, transcendentals=0),
        name="pair_bias",
    )(pair, gain.reshape(1, C), weight.T)


def grad_kernel(part_ref, bias_ref, inv_ref, hat_ref, weight_ref, out_ref, y_s):
    rows, width, chan = out_ref.shape
    heads = bias_ref.shape[0]
    copies = part_ref.shape[0] // heads
    pitch = width + 1
    grads = part_ref[...].astype(F32).reshape(heads, copies, width, rows).sum(axis=1)
    inv = inv_ref[...]
    tilt = jnp.sum(grads * bias_ref[:, 0].astype(F32), axis=0) * (inv * (1.0 / chan))
    grads = grads * inv[None]
    for g in range(width // GROUP):
        part = grads[:, g * GROUP:(g + 1) * GROUP, :].reshape(heads * GROUP, rows)
        hi, lo = split(part)
        scaled = jnp.dot(weight_ref[...], jnp.concatenate([hi, lo, hi], 0), preferred_element_type=F32)
        for n in range(GROUP):
            j = g * GROUP + n
            d = scaled[n * chan:(n + 1) * chan] - tilt[j:j + 1, :] * hat_ref[j].astype(F32)
            y_s[pl.ds(j, rows, stride=pitch), :] = d.astype(BF16).T.astype(F32)
    for i in range(rows):
        out_ref[i] = y_s[i * pitch:i * pitch + width, :].astype(BF16)


def pair_grad(parts, bias, inv, hat, weight, block=256):
    W, C, I = hat.shape
    H, copies = bias.shape[:2]
    whole = lambda a: pl.BlockSpec(a.shape, lambda n: (0,) * a.ndim)
    return pl.pallas_call(
        grad_kernel,
        grid=(I // block,),
        in_specs=[pl.BlockSpec((H * copies, W, block), lambda n: (0, 0, n)),
                  pl.BlockSpec((H, 1, W, block), lambda n: (0, 0, 0, n)),
                  pl.BlockSpec((W, block), lambda n: (0, n)),
                  pl.BlockSpec((W, C, block), lambda n: (0, 0, n)),
                  whole(weight)],
        out_specs=pl.BlockSpec((block, W, C), lambda n: (n, 0, 0)),
        out_shape=jax.ShapeDtypeStruct((I, W, C), BF16),
        scratch_shapes=[pltpu.VMEM((block * (W + 1), C), F32)],
        compiler_params=pltpu.CompilerParams(vmem_limit_bytes=32 * 1024 * 1024),
        cost_estimate=pl.CostEstimate(flops=10 << 30, bytes_accessed=20 << 20, transcendentals=0),
        name="pair_grad",
    )(parts, bias, inv, hat, weight)


def grad_weight(weight, gain):
    scaled = weight.astype(F32) * gain[:, None]
    hi, lo = split((scaled - jnp.mean(scaled, axis=0, keepdims=True)).T)
    return jnp.concatenate([spread(w.astype(F32)).astype(BF16) for w in (hi, hi, lo)], 0).T


def attend_kernel(core_ref, mine_ref, other_ref, mask_ref, q_ref, k_ref, v_ref, g_ref,
                  o_ref, dq_ref, keep_ref, send_ref,
                  bias_s, acc_s, s0_s, s1_s, e0_s, e1_s, kt_s, vt_s, kc_s, g2_s, mask_s):
    step = pl.program_id(0)
    steps = pl.num_programs(0)
    n_i = q_ref.shape[-1]
    dh = q_ref.shape[-2]
    n_j = bias_s.shape[0]
    rows = k_ref.shape[0]
    per = JT = n_j // rows
    core = core_ref[0]
    blocks = mine_ref.shape[0]
    bj = mine_ref.shape[1]
    scaling = 1.0 / math.sqrt(dh)
    IH = n_i // 2
    half = (slice(0, IH), slice(IH, 2 * IH))
    s_s = (s0_s, s1_s)
    e_s = (e0_s, e1_s)

    def position(b, parity):
        return pl.ds(pl.multiple_of((b * 2 + parity) * bj, bj), bj)

    @pl.when(step == 0)
    def _():
        mask_s[...] = jnp.concatenate([mask_ref[r, 0, :16, :].astype(F32) for r in range(rows)], 1).T

        @pl.loop(0, blocks, unroll=4)
        def _(b):
            for src, par in ((mine_ref, core), (other_ref, 1 - core)):
                at = position(b, par)
                bias_s[at, :] = jnp.where(mask_s[at, 0:1] > 0, src[b].astype(F32) * LOG2E, NEG)
                acc_s[at, :] = jnp.zeros((bj, n_i), F32)

        e1_s[...] = jnp.zeros_like(e1_s)
        vt_s[...] = jnp.zeros_like(vt_s)
        g2_s[...] = jnp.zeros_like(g2_s)
        kc_s[...] = jnp.zeros_like(kc_s)

    tiles = range(0, n_j, JT)

    def scores(h):
        il = half[h]
        q = q_ref[0, :, il].astype(F32) * (scaling * LOG2E)
        qh = q.astype(BF16)
        ql = (q - qh.astype(F32)).astype(BF16)
        q2 = jnp.concatenate([qh, ql], 0)
        m = None
        for t in tiles:
            s = jnp.dot(kt_s[t:t + JT, :], q2, preferred_element_type=F32) + bias_s[t:t + JT, il]
            s_s[h][t:t + JT, :] = s
            mt = jnp.max(s.reshape(JT // 8, 8, IH), axis=0)
            m = mt if m is None else jnp.maximum(m, mt)
            yield None
        yield jnp.max(m, axis=0, keepdims=True)

    def soften(h, m):
        il = half[h]
        o = None
        one = jnp.ones((16, JT), BF16)
        for t in tiles:
            e = jnp.exp2(s_s[h][t:t + JT, :] - m).astype(BF16)
            e_s[h][t:t + JT, :] = e
            v = v_ref[t // per, 0]
            ot = jnp.dot(jnp.concatenate([v, one], 0), e, preferred_element_type=F32)
            o = ot if o is None else o + ot
            yield None
        inv = 1.0 / o[dh:dh + 1, :]
        o = o[:dh] * inv
        o_ref[0, :, il] = o.astype(BF16)
        g = g_ref[0, :, il].astype(F32)
        centre = jnp.sum(g * o, axis=0, keepdims=True)
        g = g * inv
        c = -centre * inv
        gh = g.astype(BF16)
        gl = (g - gh.astype(F32)).astype(BF16)
        ch = c.astype(BF16).astype(F32)
        cl = c - ch
        line = lax.broadcasted_iota(jnp.int32, (16, IH), 0)
        cb = jnp.where(line == 0, ch, jnp.where(line == 1, cl, 0.0)).astype(BF16)
        yield jnp.concatenate([gh, gl, cb], 0)

    def backward(h, at, g2):
        il = half[h]
        dq = None
        for t in tiles:
            x = jnp.dot(vt_s[t:t + JT, :], g2, preferred_element_type=F32)
            ds = e_s[h][t:t + JT, :].astype(F32) * x
            acc_s[t:t + JT, il] += ds
            dt = jnp.dot(kc_s[:, t:t + JT], ds.astype(BF16), preferred_element_type=F32)
            dq = dt if dq is None else dq + dt
            yield None
        dq_ref[at, :, il] = (dq * scaling).astype(BF16)
        yield None

    def together(*chains):
        last = [None] * len(chains)
        live = list(range(len(chains)))
        while live:
            for n in list(live):
                try:
                    last[n] = next(chains[n])
                except StopIteration:
                    live.remove(n)
        return last

    for r in range(rows):
        sl = slice(r * per, (r + 1) * per)
        kz = k_ref[r, 0] * mask_ref[r, 0]
        kt_s[sl, :] = jnp.concatenate([kz, kz], 0).T
    m0, _ = together(scores(0), backward(1, jnp.maximum(step - 1, 0), g2_s[...]))
    for r in range(rows):
        sl = slice(r * per, (r + 1) * per)
        v = v_ref[r, 0]
        vt_s[sl, :] = jnp.concatenate([v, v, jnp.ones((16, per), BF16)], 0).T
        kc_s[:, sl] = k_ref[r, 0]
    g20, m1 = together(soften(0, m0), scores(1))
    _, g21 = together(backward(0, step, g20), soften(1, m1))
    g2_s[...] = g21

    @pl.when(step == steps - 1)
    def _():
        together(backward(1, step, g2_s[...]))

        @pl.loop(0, blocks, unroll=4)
        def _(b):
            for dst, par in ((keep_ref, core), (send_ref, 1 - core)):
                dst[b] = acc_s[position(b, par), :].astype(BF16)


def attention(core, mine, other, q, kv, g):
    S, dh, I = q.shape
    R, per = kv.shape[0], kv.shape[3]
    J = R * per
    IH = I // 2
    full = lambda a: pl.BlockSpec(a.shape, lambda s: (0,) * a.ndim)
    one = pl.BlockSpec((1, dh, I), lambda s: (s, 0, 0))
    all_rows = lambda at: pl.BlockSpec((R, 1, dh, per), lambda s: (0, at(s), 0, 0))
    return pl.pallas_call(
        attend_kernel,
        grid=(S,),
        in_specs=[pl.BlockSpec(memory_space=pltpu.SMEM), full(mine), full(other), all_rows(lambda s: 2 * S),
                  one, all_rows(lambda s: s), all_rows(lambda s: s + S), one],
        out_specs=[one, full(q), full(mine), full(other)],
        out_shape=[jax.ShapeDtypeStruct(a.shape, BF16) for a in (q, q, mine, other)],
        scratch_shapes=[pltpu.VMEM((J, I), F32), pltpu.VMEM((J, I), F32),
                        pltpu.VMEM((J, IH), F32), pltpu.VMEM((J, IH), F32),
                        pltpu.VMEM((J, IH), BF16), pltpu.VMEM((J, IH), BF16),
                        pltpu.VMEM((J, 2 * dh), BF16), pltpu.VMEM((J, 2 * dh + 16), BF16),
                        pltpu.VMEM((dh, J), BF16), pltpu.VMEM((2 * dh + 16, IH), BF16),
                        pltpu.VMEM((J, 16), F32)],
        compiler_params=pltpu.CompilerParams(vmem_limit_bytes=32 * 1024 * 1024),
        cost_estimate=pl.CostEstimate(flops=8 * S * J * I * dh, bytes_accessed=12 << 20, transcendentals=S * I * J),
        name="attend",
    )(core, mine, other, kv, q, kv, kv, g)


def pack_kernel(k_ref, v_ref, m_ref, out_ref):
    S = k_ref.shape[0]
    out_ref[:S] = k_ref[...]
    out_ref[S:2 * S] = v_ref[...]
    out_ref[2 * S] = jnp.broadcast_to(m_ref[...].astype(F32), out_ref.shape[1:]).astype(BF16)


def pack(k, v, mask):
    S, dh, per = k.shape
    return pl.pallas_call(
        pack_kernel,
        out_shape=jax.ShapeDtypeStruct((2 * S + 1, dh, per), BF16),
        compiler_params=pltpu.CompilerParams(vmem_limit_bytes=8 * 1024 * 1024),
        name="pack",
    )(k, v, mask.reshape(1, per))


def local(pair, pair_gain, pair_weight, queries, keys, values, d_atoms, key_mask, atom_token):
    strip = queries.shape[3]
    swap = lambda x: lax.ppermute(x, "core", [(0, 1), (1, 0)])
    spread_out = lambda x: lax.all_to_all(x, ("col", "zhi"), 0, 0, tiled=True)

    kv = lax.all_gather(pack(keys[:, 0], values[:, 0], key_mask), "row")
    bias, hat, inv = pair_bias(pair, pair_gain, pair_weight, lax.axis_size("zhi"))
    heads, copies, width, _ = bias.shape
    mine = spread_out(bias.reshape(heads * copies, width, strip))
    other = swap(mine)

    offset = lax.axis_index("row") * strip
    onehot = (
        atom_token[:, None] - offset == jnp.arange(strip, dtype=jnp.int32)[None, :]
    ).astype(BF16)
    grad_out = jnp.einsum(
        "sda,at->sdt", d_atoms[:, 0], onehot, preferred_element_type=F32
    ).astype(BF16)

    core = lax.axis_index("core").astype(jnp.int32).reshape(1)
    weight = grad_weight(pair_weight, pair_gain)
    kv, weight = lax.optimization_barrier((kv, weight))
    o, dq, keep, send = attention(core, mine, other, queries[:, 0], kv, grad_out)

    chip = (keep.astype(F32) + swap(send).astype(F32)).astype(BF16)
    d_pair = pair_grad(spread_out(chip), bias, inv, hat, weight)
    return (o[:, None], dq[:, None], d_pair)


def solution(mesh):
    fine = Mesh(mesh.devices.reshape(4, 16, 2, 2), ("row", "col", "zhi", "core"))
    sample = ("zhi", "core")
    tokens = P(sample, "col", None, "row")
    tile = P("row", ("col", "zhi", "core"), None)
    return jax.shard_map(
        local,
        mesh=fine,
        in_specs=(tile, P(), P(), tokens, tokens, tokens, tokens, P("row"), P("row")),
        out_specs=(tokens, tokens, tile),
        check_vma=False,
    )
```

```python
import math

import jax
import jax.numpy as jnp
from jax import lax
from jax.experimental import pallas as pl
from jax.experimental.pallas import tpu as pltpu
from jax.sharding import Mesh, PartitionSpec as P

F32, BF16 = jnp.float32, jnp.bfloat16
EPS = 1e-05
LOG2E = 1.4426950408889634
NEG = -1e9
GROUP = 8
MASK = 16
VMEM = 60 * 1024 * 1024


def split(x):
    hi = x.astype(BF16)
    return hi, (x - hi.astype(F32)).astype(BF16)


def spread(w):
    rows, c = w.shape
    tall = jnp.broadcast_to(w[:, None, :], (rows, GROUP, c)).reshape(rows * GROUP, c)
    line = lax.broadcasted_iota(jnp.int32, tall.shape, 0) % GROUP
    return jnp.concatenate([jnp.where(line == j, tall, 0.0) for j in range(GROUP)], 1)


def turned(pair_ref, x_s):
    rows, width, chan = pair_ref.shape
    pitch = width + 1
    for i in range(rows):
        x_s[i * pitch:i * pitch + width, :] = pair_ref[i].astype(F32)
    for j in range(width):
        x = x_s[pl.ds(j, rows, stride=pitch), :].astype(BF16).T.astype(F32)
        cen = x - jnp.mean(x, axis=0, keepdims=True)
        inv = lax.rsqrt(jnp.mean(cen * cen, axis=0, keepdims=True) + EPS)
        yield j, cen * inv, inv


def bias_kernel(pair_ref, gain_ref, weight_ref, out_ref, x_s):
    rows, width, chan = pair_ref.shape
    heads, copies = out_ref.shape[:2]
    gain = jnp.broadcast_to(gain_ref[...], (GROUP, chan)).T[:, 0:1]
    weight = spread(weight_ref[...].astype(F32)).astype(BF16)
    cols, found = [], []
    for j, hat, _ in turned(pair_ref, x_s):
        cols.append((hat * gain).astype(BF16))
        if len(cols) == GROUP:
            tile = jnp.dot(weight, jnp.concatenate(cols, 0), preferred_element_type=F32)
            found.append(tile.reshape(heads, GROUP, rows))
            cols = []
        if len(found) == 2:
            both = jnp.concatenate(found, 1).astype(BF16)
            for z in range(copies):
                out_ref[:, z, j + 1 - 2 * GROUP:j + 1, :] = both
            found = []


def pair_bias(pair, gain, weight, copies, block=256):
    I, W, C = pair.shape
    H = weight.shape[1]
    return pl.pallas_call(
        bias_kernel,
        grid=(I // block,),
        in_specs=[pl.BlockSpec((block, W, C), lambda n: (n, 0, 0)),
                  pl.BlockSpec((1, C), lambda n: (0, 0)),
                  pl.BlockSpec((H, C), lambda n: (0, 0))],
        out_specs=pl.BlockSpec((H, copies, W, block), lambda n: (0, 0, 0, n)),
        out_shape=jax.ShapeDtypeStruct((H, copies, W, I), BF16),
        scratch_shapes=[pltpu.VMEM((block * (W + 1), C), F32)],
        compiler_params=pltpu.CompilerParams(vmem_limit_bytes=VMEM),
        cost_estimate=pl.CostEstimate(flops=20 << 30, bytes_accessed=40 << 20, transcendentals=0),
        name="pair_bias",
    )(pair, gain.reshape(1, C), weight.T)


def hat_kernel(pair_ref, hat_ref, inv_ref, x_s):
    for j, hat, inv in turned(pair_ref, x_s):
        hat_ref[j] = hat.astype(BF16)
        inv_ref[j:j + 1, :] = inv


def pair_hat(pair, block=256):
    I, W, C = pair.shape
    return pl.pallas_call(
        hat_kernel,
        grid=(I // block,),
        in_specs=[pl.BlockSpec((block, W, C), lambda n: (n, 0, 0))],
        out_specs=[pl.BlockSpec((W, C, block), lambda n: (0, 0, n)),
                   pl.BlockSpec((W, block), lambda n: (0, n))],
        out_shape=[jax.ShapeDtypeStruct((W, C, I), BF16), jax.ShapeDtypeStruct((W, I), F32)],
        scratch_shapes=[pltpu.VMEM((block * (W + 1), C), F32)],
        compiler_params=pltpu.CompilerParams(vmem_limit_bytes=VMEM),
        cost_estimate=pl.CostEstimate(flops=4 << 30, bytes_accessed=20 << 20, transcendentals=0),
        name="pair_hat",
    )(pair)


def grad_kernel(part_ref, bias_ref, inv_ref, hat_ref, weight_ref, out_ref, y_s):
    rows, width, chan = out_ref.shape
    heads = bias_ref.shape[0]
    copies = part_ref.shape[0] // heads
    pitch = width + 1
    grads = part_ref[...].astype(F32).reshape(heads, copies, width, rows).sum(axis=1)
    inv = inv_ref[...]
    tilt = jnp.sum(grads * bias_ref[:, 0].astype(F32), axis=0) * (inv * (1.0 / chan))
    grads = grads * inv[None]
    for g in range(width // GROUP):
        part = grads[:, g * GROUP:(g + 1) * GROUP, :].reshape(heads * GROUP, rows)
        hi, lo = split(part)
        scaled = jnp.dot(weight_ref[...], jnp.concatenate([hi, lo, hi], 0), preferred_element_type=F32)
        for n in range(GROUP):
            j = g * GROUP + n
            d = scaled[n * chan:(n + 1) * chan] - tilt[j:j + 1, :] * hat_ref[j].astype(F32)
            y_s[pl.ds(j, rows, stride=pitch), :] = d.astype(BF16).T.astype(F32)
    for i in range(rows):
        out_ref[i] = y_s[i * pitch:i * pitch + width, :].astype(BF16)


def pair_grad(parts, bias, inv, hat, weight, block=256):
    W, C, I = hat.shape
    H, copies = bias.shape[:2]
    whole = lambda a: pl.BlockSpec(a.shape, lambda n: (0,) * a.ndim)
    return pl.pallas_call(
        grad_kernel,
        grid=(I // block,),
        in_specs=[pl.BlockSpec((H * copies, W, block), lambda n: (0, 0, n)),
                  pl.BlockSpec((H, 1, W, block), lambda n: (0, 0, 0, n)),
                  pl.BlockSpec((W, block), lambda n: (0, n)),
                  pl.BlockSpec((W, C, block), lambda n: (0, 0, n)),
                  whole(weight)],
        out_specs=pl.BlockSpec((block, W, C), lambda n: (n, 0, 0)),
        out_shape=jax.ShapeDtypeStruct((I, W, C), BF16),
        scratch_shapes=[pltpu.VMEM((block * (W + 1), C), F32)],
        compiler_params=pltpu.CompilerParams(vmem_limit_bytes=32 * 1024 * 1024),
        cost_estimate=pl.CostEstimate(flops=10 << 30, bytes_accessed=20 << 20, transcendentals=0),
        name="pair_grad",
    )(parts, bias, inv, hat, weight)


def attend_kernel(core_ref, mine_ref, other_ref, mask_ref, q_ref, k_ref, v_ref, g_ref,
                  o_ref, dq_ref, keep_ref, send_ref,
                  bias_s, acc_s, s0_s, s1_s, e0_s, e1_s, kt_s, vt_s, kc_s, g2_s, mask_s):
    step = pl.program_id(0)
    steps = pl.num_programs(0)
    n_i = q_ref.shape[-1]
    dh = q_ref.shape[-2]
    n_j = bias_s.shape[0]
    rows = k_ref.shape[0]
    per = n_j // rows
    JT = 2 * per
    core = core_ref[0]
    blocks = mine_ref.shape[0]
    bj = mine_ref.shape[1]
    scaling = 1.0 / math.sqrt(dh)
    IH = n_i // 2
    half = (slice(0, IH), slice(IH, 2 * IH))
    s_s = (s0_s, s1_s)
    e_s = (e0_s, e1_s)

    def position(b, parity):
        return pl.ds(pl.multiple_of((b * 2 + parity) * bj, bj), bj)

    @pl.when(step == 0)
    def _():
        mask_s[...] = jnp.concatenate([mask_ref[r].astype(F32) for r in range(rows)], 1).T

        @pl.loop(0, blocks, unroll=4)
        def _(b):
            for src, par in ((mine_ref, core), (other_ref, 1 - core)):
                at = position(b, par)
                bias_s[at, :] = jnp.where(mask_s[at, 0:1] > 0, src[b].astype(F32) * LOG2E, NEG)
                acc_s[at, :] = jnp.zeros((bj, n_i), F32)

        e1_s[...] = jnp.zeros_like(e1_s)
        vt_s[...] = jnp.zeros_like(vt_s)
        g2_s[...] = jnp.zeros_like(g2_s)
        kc_s[...] = jnp.zeros_like(kc_s)

    tiles = range(0, n_j, JT)

    def scores(h):
        il = half[h]
        q = q_ref[0, :, il].astype(F32) * (scaling * LOG2E)
        qh = q.astype(BF16)
        ql = (q - qh.astype(F32)).astype(BF16)
        q2 = jnp.concatenate([qh, ql], 0)
        m = None
        for t in tiles:
            s = jnp.dot(kt_s[t:t + JT, :], q2, preferred_element_type=F32) + bias_s[t:t + JT, il]
            s_s[h][t:t + JT, :] = s
            mt = jnp.max(s.reshape(JT // 8, 8, IH), axis=0)
            m = mt if m is None else jnp.maximum(m, mt)
            yield None
        yield jnp.max(m, axis=0, keepdims=True)

    def soften(h, m):
        il = half[h]
        for t in tiles:
            e_s[h][t:t + JT, :] = jnp.exp2(s_s[h][t:t + JT, :] - m).astype(BF16)
            yield None
        v = jnp.concatenate([v_ref[r] for r in range(rows)], 1)
        o = jnp.dot(jnp.concatenate([v, jnp.ones((16, n_j), BF16)], 0), e_s[h][...], preferred_element_type=F32)
        yield None
        inv = 1.0 / o[dh:dh + 1, :]
        o = o[:dh] * inv
        o_ref[0, :, il] = o.astype(BF16)
        g = g_ref[0, :, il].astype(F32)
        centre = jnp.sum(g * o, axis=0, keepdims=True)
        g = g * inv
        c = -centre * inv
        gh = g.astype(BF16)
        gl = (g - gh.astype(F32)).astype(BF16)
        ch = c.astype(BF16).astype(F32)
        cl = c - ch
        line = lax.broadcasted_iota(jnp.int32, (16, IH), 0)
        cb = jnp.where(line == 0, ch, jnp.where(line == 1, cl, 0.0)).astype(BF16)
        yield jnp.concatenate([gh, gl, cb], 0)

    def backward(h, at, g2):
        il = half[h]
        dq = None
        for t in tiles:
            x = jnp.dot(vt_s[t:t + JT, :], g2, preferred_element_type=F32)
            ds = e_s[h][t:t + JT, :].astype(F32) * x
            acc_s[t:t + JT, il] += ds
            dt = jnp.dot(kc_s[:, t:t + JT], ds.astype(BF16), preferred_element_type=F32)
            dq = dt if dq is None else dq + dt
            yield None
        dq_ref[at, :, il] = (dq * scaling).astype(BF16)
        yield None

    def together(*chains):
        last = [None] * len(chains)
        live = list(range(len(chains)))
        while live:
            for n in list(live):
                try:
                    last[n] = next(chains[n])
                except StopIteration:
                    live.remove(n)
        return last

    for r in range(rows):
        sl = slice(r * per, (r + 1) * per)
        kz = k_ref[r] * mask_ref[r, 0:1, :]
        kt_s[sl, :] = jnp.concatenate([kz, kz], 0).T
    m0, _ = together(scores(0), backward(1, jnp.maximum(step - 1, 0), g2_s[...]))
    for r in range(rows):
        sl = slice(r * per, (r + 1) * per)
        v = v_ref[r]
        vt_s[sl, :] = jnp.concatenate([v, v, jnp.ones((16, per), BF16)], 0).T
        kc_s[:, sl] = k_ref[r]
    g20, m1 = together(soften(0, m0), scores(1))
    _, g21 = together(backward(0, step, g20), soften(1, m1))
    g2_s[...] = g21

    @pl.when(step == steps - 1)
    def _():
        together(backward(1, step, g2_s[...]))

        @pl.loop(0, blocks, unroll=4)
        def _(b):
            for dst, par in ((keep_ref, core), (send_ref, 1 - core)):
                dst[b] = acc_s[position(b, par), :].astype(BF16)


def attention(core, mine, other, q, kv, g):
    S, dh, I = q.shape
    R, per = kv.shape[0], kv.shape[2]
    J = R * per
    IH = I // 2
    full = lambda a: pl.BlockSpec(a.shape, lambda s: (0,) * a.ndim)
    one = pl.BlockSpec((1, dh, I), lambda s: (s, 0, 0))
    all_rows = lambda n, at: pl.BlockSpec((R, n, per), lambda s: (0, at(s), 0))
    return pl.pallas_call(
        attend_kernel,
        grid=(S,),
        in_specs=[pl.BlockSpec(memory_space=pltpu.SMEM), full(mine), full(other), all_rows(MASK, lambda s: 2 * S * dh // MASK),
                  one, all_rows(dh, lambda s: s), all_rows(dh, lambda s: s + S), one],
        out_specs=[one, full(q), full(mine), full(other)],
        out_shape=[jax.ShapeDtypeStruct(a.shape, BF16) for a in (q, q, mine, other)],
        scratch_shapes=[pltpu.VMEM((J, I), F32), pltpu.VMEM((J, I), F32),
                        pltpu.VMEM((J, IH), F32), pltpu.VMEM((J, IH), F32),
                        pltpu.VMEM((J, IH), BF16), pltpu.VMEM((J, IH), BF16),
                        pltpu.VMEM((J, 2 * dh), BF16), pltpu.VMEM((J, 2 * dh + 16), BF16),
                        pltpu.VMEM((dh, J), BF16), pltpu.VMEM((2 * dh + 16, IH), BF16),
                        pltpu.VMEM((J, 16), F32)],
        compiler_params=pltpu.CompilerParams(vmem_limit_bytes=61 * 1024 * 1024),
        input_output_aliases={1: 2, 2: 3},
        cost_estimate=pl.CostEstimate(flops=8 * S * J * I * dh, bytes_accessed=12 << 20, transcendentals=S * I * J),
        name="attend",
    )(core, mine, other, kv, q, kv, kv, g)


def pack_kernel(k_ref, v_ref, m_ref, out_ref):
    S, dh, per = k_ref.shape
    out_ref[:S * dh] = k_ref[...].reshape(S * dh, per)
    out_ref[S * dh:2 * S * dh] = v_ref[...].reshape(S * dh, per)
    out_ref[2 * S * dh:] = jnp.broadcast_to(m_ref[...].astype(F32), (MASK, per)).astype(BF16)


def pack(k, v, mask):
    S, dh, per = k.shape
    return pl.pallas_call(
        pack_kernel,
        out_shape=jax.ShapeDtypeStruct((2 * S * dh + MASK, per), BF16),
        compiler_params=pltpu.CompilerParams(vmem_limit_bytes=VMEM),
        name="pack",
    )(k, v, mask.reshape(1, per))


def weight_kernel(weight_ref, gain_ref, out_ref):
    scaled = weight_ref[...].astype(F32) * gain_ref[...]
    hi, lo = (x.astype(F32) for x in split(scaled - jnp.mean(scaled, axis=1, keepdims=True)))
    out_ref[...] = jnp.concatenate([spread(w) for w in (hi, hi, lo)], 0).T.astype(BF16)


def grad_weight(weight, gain):
    C, H = weight.shape
    return pl.pallas_call(
        weight_kernel,
        out_shape=jax.ShapeDtypeStruct((GROUP * C, 3 * H * GROUP), BF16),
        compiler_params=pltpu.CompilerParams(vmem_limit_bytes=32 * 1024 * 1024),
        name="grad_weight",
    )(weight.T, gain.reshape(1, C))


def local(pair, pair_gain, pair_weight, queries, keys, values, d_atoms, key_mask, atom_token):
    strip = queries.shape[3]
    swap = lambda x: lax.ppermute(x, "core", [(0, 1), (1, 0)])
    spread_out = lambda x: lax.all_to_all(x, ("col", "zhi"), 0, 0, tiled=True)

    kv = lax.all_gather(pack(keys[:, 0], values[:, 0], key_mask), "row")
    bias = pair_bias(pair, pair_gain, pair_weight, lax.axis_size("zhi"))
    heads, copies, width, _ = bias.shape
    mine = spread_out(bias.reshape(heads * copies, width, strip))
    other = swap(mine)

    offset = lax.axis_index("row") * strip
    onehot = (
        atom_token[:, None] - offset == jnp.arange(strip, dtype=jnp.int32)[None, :]
    ).astype(BF16)
    grad_out = jnp.einsum(
        "sda,at->sdt", d_atoms[:, 0], onehot, preferred_element_type=F32
    ).astype(BF16)

    core = lax.axis_index("core").astype(jnp.int32).reshape(1)
    weight = grad_weight(pair_weight, pair_gain)
    kv, grad_out, weight = lax.optimization_barrier((kv, grad_out, weight))
    o, dq, keep, send = attention(core, mine, other, queries[:, 0], kv, grad_out)

    chip = (keep.astype(F32) + swap(send).astype(F32)).astype(BF16)
    chip, pair = lax.optimization_barrier((chip, pair))
    parts = spread_out(chip)
    hat, inv = pair_hat(pair)
    d_pair = pair_grad(parts, bias, inv, hat, weight)
    return (o[:, None], dq[:, None], d_pair)


def solution(mesh):
    fine = Mesh(mesh.devices.reshape(4, 16, 2, 2), ("row", "col", "zhi", "core"))
    sample = ("zhi", "core")
    tokens = P(sample, "col", None, "row")
    tile = P("row", ("col", "zhi", "core"), None)
    return jax.shard_map(
        local,
        mesh=fine,
        in_specs=(tile, P(), P(), tokens, tokens, tokens, tokens, P("row"), P("row")),
        out_specs=(tokens, tokens, tile),
        check_vma=False,
    )
```

```python
import functools
import math

import jax
import jax.numpy as jnp
from jax import lax
from jax.experimental import pallas as pl
from jax.experimental.pallas import tpu as pltpu
from jax.sharding import Mesh, PartitionSpec as P

F32, BF16 = jnp.float32, jnp.bfloat16
EPS = 1e-05
LOG2E = 1.4426950408889634
NEG = -1e9
GROUP = 8
MASK = 16
VMEM = 60 * 1024 * 1024


def split(x):
    hi = x.astype(BF16)
    return hi, (x - hi.astype(F32)).astype(BF16)


def spread(w):
    rows, c = w.shape
    tall = jnp.broadcast_to(w[:, None, :], (rows, GROUP, c)).reshape(rows * GROUP, c)
    line = lax.broadcasted_iota(jnp.int32, tall.shape, 0) % GROUP
    return jnp.concatenate([jnp.where(line == j, tall, 0.0) for j in range(GROUP)], 1)


def turned(pair_ref, x_s):
    rows, width, chan = pair_ref.shape
    pitch = width + 1
    for i in range(rows):
        x_s[i * pitch:i * pitch + width, :] = pair_ref[i].astype(F32)
    for j in range(width):
        x = x_s[pl.ds(j, rows, stride=pitch), :].astype(BF16).T.astype(F32)
        cen = x - jnp.mean(x, axis=0, keepdims=True)
        inv = lax.rsqrt(jnp.mean(cen * cen, axis=0, keepdims=True) + EPS)
        yield j, cen * inv, inv


def bias_kernel(pair_ref, gain_ref, weight_ref, out_ref, x_s):
    rows, width, chan = pair_ref.shape
    heads, copies = out_ref.shape[:2]
    gain = jnp.broadcast_to(gain_ref[...], (GROUP, chan)).T[:, 0:1]
    weight = spread(weight_ref[...].astype(F32)).astype(BF16)
    cols, found = [], []
    for j, hat, _ in turned(pair_ref, x_s):
        cols.append((hat * gain).astype(BF16))
        if len(cols) == GROUP:
            tile = jnp.dot(weight, jnp.concatenate(cols, 0), preferred_element_type=F32)
            found.append(tile.reshape(heads, GROUP, rows))
            cols = []
        if len(found) == 2:
            both = jnp.concatenate(found, 1).astype(BF16)
            for z in range(copies):
                out_ref[:, z, j + 1 - 2 * GROUP:j + 1, :] = both
            found = []


def pair_bias(pair, gain, weight, copies, block=256):
    I, W, C = pair.shape
    H = weight.shape[1]
    return pl.pallas_call(
        bias_kernel,
        grid=(I // block,),
        in_specs=[pl.BlockSpec((block, W, C), lambda n: (n, 0, 0)),
                  pl.BlockSpec((1, C), lambda n: (0, 0)),
                  pl.BlockSpec((H, C), lambda n: (0, 0))],
        out_specs=pl.BlockSpec((H, copies, W, block), lambda n: (0, 0, 0, n)),
        out_shape=jax.ShapeDtypeStruct((H, copies, W, I), BF16),
        scratch_shapes=[pltpu.VMEM((block * (W + 1), C), F32)],
        compiler_params=pltpu.CompilerParams(vmem_limit_bytes=VMEM),
        cost_estimate=pl.CostEstimate(flops=100 << 30, bytes_accessed=40 << 20, transcendentals=0),
        name="pair_bias",
    )(pair, gain.reshape(1, C), weight.T)


def hat_kernel(pair_ref, hat_ref, inv_ref, x_s):
    for j, hat, inv in turned(pair_ref, x_s):
        hat_ref[j] = hat.astype(BF16)
        inv_ref[j:j + 1, :] = inv


def pair_hat(pair, block=256):
    I, W, C = pair.shape
    return pl.pallas_call(
        hat_kernel,
        grid=(I // block,),
        in_specs=[pl.BlockSpec((block, W, C), lambda n: (n, 0, 0))],
        out_specs=[pl.BlockSpec((W, C, block), lambda n: (0, 0, n)),
                   pl.BlockSpec((W, block), lambda n: (0, n))],
        out_shape=[jax.ShapeDtypeStruct((W, C, I), BF16), jax.ShapeDtypeStruct((W, I), F32)],
        scratch_shapes=[pltpu.VMEM((block * (W + 1), C), F32)],
        compiler_params=pltpu.CompilerParams(vmem_limit_bytes=VMEM),
        cost_estimate=pl.CostEstimate(flops=400 << 30, bytes_accessed=20 << 20, transcendentals=0),
        name="pair_hat",
    )(pair)


def grad_kernel(part_ref, bias_ref, inv_ref, hat_ref, weight_ref, out_ref, y_s):
    rows, width, chan = out_ref.shape
    heads = bias_ref.shape[0]
    copies = part_ref.shape[0] // heads
    pitch = width + 1
    grads = part_ref[...].astype(F32).reshape(heads, copies, width, rows).sum(axis=1)
    inv = inv_ref[...]
    tilt = jnp.sum(grads * bias_ref[:, 0].astype(F32), axis=0) * (inv * (1.0 / chan))
    grads = grads * inv[None]
    for g in range(width // GROUP):
        part = grads[:, g * GROUP:(g + 1) * GROUP, :].reshape(heads * GROUP, rows)
        hi, lo = split(part)
        scaled = jnp.dot(weight_ref[...], jnp.concatenate([hi, lo, hi], 0), preferred_element_type=F32)
        for n in range(GROUP):
            j = g * GROUP + n
            d = scaled[n * chan:(n + 1) * chan] - tilt[j:j + 1, :] * hat_ref[j].astype(F32)
            y_s[pl.ds(j, rows, stride=pitch), :] = d.astype(BF16).T.astype(F32)
    for i in range(rows):
        out_ref[i] = y_s[i * pitch:i * pitch + width, :].astype(BF16)


def pair_grad(parts, bias, inv, hat, weight, block=256):
    W, C, I = hat.shape
    H, copies = bias.shape[:2]
    whole = lambda a: pl.BlockSpec(a.shape, lambda n: (0,) * a.ndim)
    return pl.pallas_call(
        grad_kernel,
        grid=(I // block,),
        in_specs=[pl.BlockSpec((H * copies, W, block), lambda n: (0, 0, n)),
                  pl.BlockSpec((H, 1, W, block), lambda n: (0, 0, 0, n)),
                  pl.BlockSpec((W, block), lambda n: (0, n)),
                  pl.BlockSpec((W, C, block), lambda n: (0, 0, n)),
                  whole(weight)],
        out_specs=pl.BlockSpec((block, W, C), lambda n: (n, 0, 0)),
        out_shape=jax.ShapeDtypeStruct((I, W, C), BF16),
        scratch_shapes=[pltpu.VMEM((block * (W + 1), C), F32)],
        compiler_params=pltpu.CompilerParams(vmem_limit_bytes=32 * 1024 * 1024),
        cost_estimate=pl.CostEstimate(flops=10 << 30, bytes_accessed=20 << 20, transcendentals=0),
        name="pair_grad",
    )(parts, bias, inv, hat, weight)


def attend_kernel(rows, place_ref, mine_ref, other_ref, q_ref, g_ref, *refs):
    k_refs, v_refs, mask_refs = refs[:rows], refs[rows:2 * rows], refs[2 * rows:3 * rows]
    attend_body(place_ref, mine_ref, other_ref, q_ref, g_ref, k_refs, v_refs, mask_refs, *refs[3 * rows:])


def attend_body(place_ref, mine_ref, other_ref, q_ref, g_ref, k_refs, v_refs, mask_refs,
                o_ref, dq_ref, keep_ref, send_ref,
                bias_s, acc_s, s0_s, s1_s, e0_s, e1_s, kt_s, vt_s, kc_s, g2_s, mask_s):
    step = pl.program_id(0)
    steps = pl.num_programs(0)
    n_i = q_ref.shape[-1]
    dh = q_ref.shape[-2]
    n_j = bias_s.shape[0]
    rows = len(k_refs)
    per = n_j // rows
    JT = 2 * per
    core = place_ref[0]
    row = place_ref[1]
    blocks = mine_ref.shape[0]
    bj = mine_ref.shape[1]
    scaling = 1.0 / math.sqrt(dh)
    IH = n_i // 2
    half = (slice(0, IH), slice(IH, 2 * IH))
    s_s = (s0_s, s1_s)
    e_s = (e0_s, e1_s)

    def position(b, parity):
        token = (b * 2 + parity) * bj
        token = (token // per + rows - row) % rows * per + token % per
        return pl.ds(pl.multiple_of(token, bj), bj)

    @pl.when(step == 0)
    def _():
        mask_s[...] = jnp.concatenate([mask_refs[r][...].astype(F32) for r in range(rows)], 1).T

        @pl.loop(0, blocks, unroll=4)
        def _(b):
            for src, par in ((mine_ref, core), (other_ref, 1 - core)):
                at = position(b, par)
                bias_s[at, :] = jnp.where(mask_s[at, 0:1] > 0, src[b].astype(F32) * LOG2E, NEG)
                acc_s[at, :] = jnp.zeros((bj, n_i), F32)

        e1_s[...] = jnp.zeros_like(e1_s)
        vt_s[...] = jnp.zeros_like(vt_s)
        g2_s[...] = jnp.zeros_like(g2_s)
        kc_s[...] = jnp.zeros_like(kc_s)

    tiles = range(0, n_j, JT)

    def scores(h):
        il = half[h]
        q = q_ref[0, :, il].astype(F32) * (scaling * LOG2E)
        qh = q.astype(BF16)
        ql = (q - qh.astype(F32)).astype(BF16)
        q2 = jnp.concatenate([qh, ql], 0)
        m = None
        for t in tiles:
            s = jnp.dot(kt_s[t:t + JT, :], q2, preferred_element_type=F32) + bias_s[t:t + JT, il]
            s_s[h][t:t + JT, :] = s
            mt = jnp.max(s.reshape(JT // 8, 8, IH), axis=0)
            m = mt if m is None else jnp.maximum(m, mt)
            yield None
        yield jnp.max(m, axis=0, keepdims=True)

    def soften(h, m):
        il = half[h]
        for t in tiles:
            e_s[h][t:t + JT, :] = jnp.exp2(s_s[h][t:t + JT, :] - m).astype(BF16)
            yield None
        v = jnp.concatenate([v_refs[r][...] for r in range(rows)], 1)
        o = jnp.dot(jnp.concatenate([v, jnp.ones((16, n_j), BF16)], 0), e_s[h][...], preferred_element_type=F32)
        yield None
        inv = 1.0 / o[dh:dh + 1, :]
        o = o[:dh] * inv
        o_ref[0, :, il] = o.astype(BF16)
        g = g_ref[0, :, il].astype(F32)
        centre = jnp.sum(g * o, axis=0, keepdims=True)
        g = g * inv
        c = -centre * inv
        gh = g.astype(BF16)
        gl = (g - gh.astype(F32)).astype(BF16)
        ch = c.astype(BF16).astype(F32)
        cl = c - ch
        line = lax.broadcasted_iota(jnp.int32, (16, IH), 0)
        cb = jnp.where(line == 0, ch, jnp.where(line == 1, cl, 0.0)).astype(BF16)
        yield jnp.concatenate([gh, gl, cb], 0)

    def backward(h, at, g2):
        il = half[h]
        dq = None
        for t in tiles:
            x = jnp.dot(vt_s[t:t + JT, :], g2, preferred_element_type=F32)
            ds = e_s[h][t:t + JT, :].astype(F32) * x
            acc_s[t:t + JT, il] += ds
            dt = jnp.dot(kc_s[:, t:t + JT], ds.astype(BF16), preferred_element_type=F32)
            dq = dt if dq is None else dq + dt
            yield None
        dq_ref[at, :, il] = (dq * scaling).astype(BF16)
        yield None

    def together(*chains):
        last = [None] * len(chains)
        live = list(range(len(chains)))
        while live:
            for n in list(live):
                try:
                    last[n] = next(chains[n])
                except StopIteration:
                    live.remove(n)
        return last

    for r in range(rows):
        sl = slice(r * per, (r + 1) * per)
        kz = k_refs[r][...] * mask_refs[r][0:1, :]
        kt_s[sl, :] = jnp.concatenate([kz, kz], 0).T
    m0, _ = together(scores(0), backward(1, jnp.maximum(step - 1, 0), g2_s[...]))
    for r in range(rows):
        sl = slice(r * per, (r + 1) * per)
        v = v_refs[r][...]
        vt_s[sl, :] = jnp.concatenate([v, v, jnp.ones((16, per), BF16)], 0).T
        kc_s[:, sl] = k_refs[r][...]
    g20, m1 = together(soften(0, m0), scores(1))
    _, g21 = together(backward(0, step, g20), soften(1, m1))
    g2_s[...] = g21

    @pl.when(step == steps - 1)
    def _():
        together(backward(1, step, g2_s[...]))

        @pl.loop(0, blocks, unroll=4)
        def _(b):
            for dst, par in ((keep_ref, core), (send_ref, 1 - core)):
                dst[b] = acc_s[position(b, par), :].astype(BF16)


def attention(place, mine, other, q, ks, vs, g):
    S, dh, I = q.shape
    R, per = len(ks), ks[0].shape[1]
    J = R * per
    IH = I // 2
    full = lambda a: pl.BlockSpec(a.shape, lambda s: (0,) * a.ndim)
    one = pl.BlockSpec((1, dh, I), lambda s: (s, 0, 0))
    own = pl.BlockSpec((dh, per), lambda s: (s, 0))
    flags = pl.BlockSpec((MASK, per), lambda s: (S * dh // MASK, 0))
    return pl.pallas_call(
        functools.partial(attend_kernel, R),
        grid=(S,),
        in_specs=[pl.BlockSpec(memory_space=pltpu.SMEM), full(mine), full(other), one, one]
        + [own] * (2 * R) + [flags] * R,
        out_specs=[one, full(q), full(mine), full(other)],
        out_shape=[jax.ShapeDtypeStruct(a.shape, BF16) for a in (q, q, mine, other)],
        scratch_shapes=[pltpu.VMEM((J, I), F32), pltpu.VMEM((J, I), F32),
                        pltpu.VMEM((J, IH), F32), pltpu.VMEM((J, IH), F32),
                        pltpu.VMEM((J, IH), BF16), pltpu.VMEM((J, IH), BF16),
                        pltpu.VMEM((J, 2 * dh), BF16), pltpu.VMEM((J, 2 * dh + 16), BF16),
                        pltpu.VMEM((dh, J), BF16), pltpu.VMEM((2 * dh + 16, IH), BF16),
                        pltpu.VMEM((J, 16), F32)],
        compiler_params=pltpu.CompilerParams(vmem_limit_bytes=121 * 512 * 1024),
        input_output_aliases={1: 2, 2: 3},
        cost_estimate=pl.CostEstimate(flops=8 * S * J * I * dh, bytes_accessed=12 << 20, transcendentals=S * I * J),
        name="attend",
    )(place, mine, other, q, g, *ks, *vs, *vs)


def pack_kernel(v_ref, m_ref, out_ref):
    S, dh, per = v_ref.shape
    out_ref[:S * dh] = v_ref[...].reshape(S * dh, per)
    out_ref[S * dh:] = jnp.broadcast_to(m_ref[...].astype(F32), (MASK, per)).astype(BF16)


def pack(v, mask):
    S, dh, per = v.shape
    return pl.pallas_call(
        pack_kernel,
        out_shape=jax.ShapeDtypeStruct((S * dh + MASK, per), BF16),
        compiler_params=pltpu.CompilerParams(vmem_limit_bytes=VMEM),
        name="pack",
    )(v, mask.reshape(1, per))


def weight_kernel(weight_ref, gain_ref, out_ref):
    scaled = weight_ref[...].astype(F32) * gain_ref[...]
    hi, lo = (x.astype(F32) for x in split(scaled - jnp.mean(scaled, axis=1, keepdims=True)))
    out_ref[...] = jnp.concatenate([spread(w) for w in (hi, hi, lo)], 0).T.astype(BF16)


def grad_weight(weight, gain):
    C, H = weight.shape
    return pl.pallas_call(
        weight_kernel,
        out_shape=jax.ShapeDtypeStruct((GROUP * C, 3 * H * GROUP), BF16),
        compiler_params=pltpu.CompilerParams(vmem_limit_bytes=32 * 1024 * 1024),
        name="grad_weight",
    )(weight.T, gain.reshape(1, C))


def local(pair, pair_gain, pair_weight, queries, keys, values, d_atoms, key_mask, atom_token):
    strip = queries.shape[3]
    swap = lambda x: lax.ppermute(x, "core", [(0, 1), (1, 0)])
    spread_out = lambda x: lax.all_to_all(x, ("col", "zhi"), 0, 0, tiled=True)

    rows = lax.axis_size("row")
    pass_on = lambda x, n: lax.ppermute(x, "row", [(i, (i + n) % rows) for i in range(rows)])
    k = keys.reshape(-1, strip)
    v = pack(values[:, 0], key_mask)
    k_behind, v_ahead = pass_on(k, 1), pass_on(v, -1)
    k_ahead, v_behind = pass_on(k, -1), pass_on(v, 1)
    k_behind, v_ahead, again = lax.optimization_barrier((k_behind, v_ahead, pair))
    hat, inv = pair_hat(again)
    k_behind, v_ahead, hat, inv = lax.optimization_barrier((k_behind, v_ahead, hat, inv))
    ks = [k, k_ahead, pass_on(k_behind, 1), k_behind]
    vs = [v, v_ahead, pass_on(v_ahead, -1), v_behind]

    bias = pair_bias(pair, pair_gain, pair_weight, lax.axis_size("zhi"))
    heads, copies, width, _ = bias.shape
    mine = spread_out(bias.reshape(heads * copies, width, strip))

    offset = lax.axis_index("row") * strip
    onehot = (
        atom_token[:, None] - offset == jnp.arange(strip, dtype=jnp.int32)[None, :]
    ).astype(BF16)
    grad_out = jnp.einsum(
        "sda,at->sdt", d_atoms[:, 0], onehot, preferred_element_type=F32
    ).astype(BF16)
    weight = grad_weight(pair_weight, pair_gain)
    mine, ks, vs, grad_out, weight, hat, inv = lax.optimization_barrier(
        (mine, ks, vs, grad_out, weight, hat, inv))
    other = swap(mine)
    place = jnp.stack([lax.axis_index("core"), lax.axis_index("row")]).astype(jnp.int32)
    o, dq, keep, send = attention(place, mine, other, queries[:, 0], ks, vs, grad_out)

    chip = (keep.astype(F32) + swap(send).astype(F32)).astype(BF16)
    d_pair = pair_grad(spread_out(chip), bias, inv, hat, weight)
    return (o[:, None], dq[:, None], d_pair)


def solution(mesh):
    fine = Mesh(mesh.devices.reshape(4, 16, 2, 2), ("row", "col", "zhi", "core"))
    sample = ("zhi", "core")
    tokens = P(sample, "col", None, "row")
    tile = P("row", ("col", "zhi", "core"), None)
    return jax.shard_map(
        local,
        mesh=fine,
        in_specs=(tile, P(), P(), tokens, tokens, tokens, tokens, P("row"), P("row")),
        out_specs=(tokens, tokens, tile),
        check_vma=False,
    )
```

```python
import functools
import math

import jax
import jax.numpy as jnp
from jax import lax
from jax.experimental import pallas as pl
from jax.experimental.pallas import tpu as pltpu
from jax.sharding import Mesh, PartitionSpec as P

F32, BF16 = jnp.float32, jnp.bfloat16
EPS = 1e-05
LOG2E = 1.4426950408889634
NEG = -1e9
GROUP = 8
MASK = 16
VMEM = 60 * 1024 * 1024


def split(x):
    hi = x.astype(BF16)
    return hi, (x - hi.astype(F32)).astype(BF16)


def spread(w):
    rows, c = w.shape
    tall = jnp.broadcast_to(w[:, None, :], (rows, GROUP, c)).reshape(rows * GROUP, c)
    line = lax.broadcasted_iota(jnp.int32, tall.shape, 0) % GROUP
    return jnp.concatenate([jnp.where(line == j, tall, 0.0) for j in range(GROUP)], 1)


def turned(pair_ref, x_s):
    rows, width, chan = pair_ref.shape
    pitch = width + 1
    for i in range(rows):
        x_s[i * pitch:i * pitch + width, :] = pair_ref[i].astype(F32)
    for j in range(width):
        x = x_s[pl.ds(j, rows, stride=pitch), :].astype(BF16).T.astype(F32)
        cen = x - jnp.mean(x, axis=0, keepdims=True)
        inv = lax.rsqrt(jnp.mean(cen * cen, axis=0, keepdims=True) + EPS)
        yield j, cen * inv, inv


def bias_kernel(pair_ref, gain_ref, weight_ref, out_ref, x_s):
    rows, width, chan = pair_ref.shape
    heads, copies = out_ref.shape[:2]
    gain = jnp.broadcast_to(gain_ref[...], (GROUP, chan)).T[:, 0:1]
    weight = spread(weight_ref[...].astype(F32)).astype(BF16)
    cols, found = [], []
    for j, hat, _ in turned(pair_ref, x_s):
        cols.append((hat * gain).astype(BF16))
        if len(cols) == GROUP:
            tile = jnp.dot(weight, jnp.concatenate(cols, 0), preferred_element_type=F32)
            found.append(tile.reshape(heads, GROUP, rows))
            cols = []
        if len(found) == 2:
            both = jnp.concatenate(found, 1).astype(BF16)
            for z in range(copies):
                out_ref[:, z, j + 1 - 2 * GROUP:j + 1, :] = both
            found = []


def pair_bias(pair, gain, weight, copies, block=256):
    I, W, C = pair.shape
    H = weight.shape[1]
    return pl.pallas_call(
        bias_kernel,
        grid=(I // block,),
        in_specs=[pl.BlockSpec((block, W, C), lambda n: (n, 0, 0)),
                  pl.BlockSpec((1, C), lambda n: (0, 0)),
                  pl.BlockSpec((H, C), lambda n: (0, 0))],
        out_specs=pl.BlockSpec((H, copies, W, block), lambda n: (0, 0, 0, n)),
        out_shape=jax.ShapeDtypeStruct((H, copies, W, I), BF16),
        scratch_shapes=[pltpu.VMEM((block * (W + 1), C), F32)],
        compiler_params=pltpu.CompilerParams(vmem_limit_bytes=VMEM),
        cost_estimate=pl.CostEstimate(flops=100 << 30, bytes_accessed=40 << 20, transcendentals=0),
        name="pair_bias",
    )(pair, gain.reshape(1, C), weight.T)


def hat_kernel(pair_ref, hat_ref, inv_ref, x_s):
    for j, hat, inv in turned(pair_ref, x_s):
        hat_ref[j] = hat.astype(BF16)
        inv_ref[j:j + 1, :] = inv


def pair_hat(pair, block=256):
    I, W, C = pair.shape
    return pl.pallas_call(
        hat_kernel,
        grid=(I // block,),
        in_specs=[pl.BlockSpec((block, W, C), lambda n: (n, 0, 0))],
        out_specs=[pl.BlockSpec((W, C, block), lambda n: (0, 0, n)),
                   pl.BlockSpec((W, block), lambda n: (0, n))],
        out_shape=[jax.ShapeDtypeStruct((W, C, I), BF16), jax.ShapeDtypeStruct((W, I), F32)],
        scratch_shapes=[pltpu.VMEM((block * (W + 1), C), F32)],
        compiler_params=pltpu.CompilerParams(vmem_limit_bytes=VMEM),
        cost_estimate=pl.CostEstimate(flops=400 << 30, bytes_accessed=20 << 20, transcendentals=0),
        name="pair_hat",
    )(pair)


def grad_kernel(part_ref, bias_ref, inv_ref, hat_ref, weight_ref, out_ref, y_s):
    rows, width, chan = out_ref.shape
    heads = bias_ref.shape[0]
    copies = part_ref.shape[0] // heads
    pitch = width + 1
    grads = part_ref[...].astype(F32).reshape(heads, copies, width, rows).sum(axis=1)
    inv = inv_ref[...]
    tilt = jnp.sum(grads * bias_ref[:, 0].astype(F32), axis=0) * (inv * (1.0 / chan))
    grads = grads * inv[None]
    for g in range(width // GROUP):
        part = grads[:, g * GROUP:(g + 1) * GROUP, :].reshape(heads * GROUP, rows)
        hi, lo = split(part)
        scaled = jnp.dot(weight_ref[...], jnp.concatenate([hi, lo, hi], 0), preferred_element_type=F32)
        for n in range(GROUP):
            j = g * GROUP + n
            d = scaled[n * chan:(n + 1) * chan] - tilt[j:j + 1, :] * hat_ref[j].astype(F32)
            y_s[pl.ds(j, rows, stride=pitch), :] = d.astype(BF16).T.astype(F32)
    for i in range(rows):
        out_ref[i] = y_s[i * pitch:i * pitch + width, :].astype(BF16)


def pair_grad(parts, bias, inv, hat, weight, block=256):
    W, C, I = hat.shape
    H, copies = bias.shape[:2]
    whole = lambda a: pl.BlockSpec(a.shape, lambda n: (0,) * a.ndim)
    return pl.pallas_call(
        grad_kernel,
        grid=(I // block,),
        in_specs=[pl.BlockSpec((H * copies, W, block), lambda n: (0, 0, n)),
                  pl.BlockSpec((H, 1, W, block), lambda n: (0, 0, 0, n)),
                  pl.BlockSpec((W, block), lambda n: (0, n)),
                  pl.BlockSpec((W, C, block), lambda n: (0, 0, n)),
                  whole(weight)],
        out_specs=pl.BlockSpec((block, W, C), lambda n: (n, 0, 0)),
        out_shape=jax.ShapeDtypeStruct((I, W, C), BF16),
        scratch_shapes=[pltpu.VMEM((block * (W + 1), C), F32)],
        compiler_params=pltpu.CompilerParams(vmem_limit_bytes=32 * 1024 * 1024),
        cost_estimate=pl.CostEstimate(flops=10 << 30, bytes_accessed=20 << 20, transcendentals=0),
        name="pair_grad",
    )(parts, bias, inv, hat, weight)


def attend_kernel(rows, place_ref, mine_ref, other_ref, q_ref, g_ref, *refs):
    k_refs, v_refs, mask_refs = refs[:rows], refs[rows:2 * rows], refs[2 * rows:3 * rows]
    attend_body(place_ref, mine_ref, other_ref, q_ref, g_ref, k_refs, v_refs, mask_refs, *refs[3 * rows:])


def attend_body(place_ref, mine_ref, other_ref, q_ref, g_ref, k_refs, v_refs, mask_refs,
                o_ref, dq_ref, keep_ref, send_ref,
                bias_s, acc_s, s0_s, s1_s, e0_s, e1_s, kt_s, vt_s, kc_s, g2_s, mask_s):
    step = pl.program_id(0)
    steps = pl.num_programs(0)
    n_i = q_ref.shape[-1]
    dh = q_ref.shape[-2]
    n_j = bias_s.shape[0]
    rows = len(k_refs)
    per = n_j // rows
    JT = 2 * per
    core = place_ref[0]
    row = place_ref[1]
    blocks = mine_ref.shape[0]
    bj = mine_ref.shape[1]
    scaling = 1.0 / math.sqrt(dh)
    IH = n_i // 2
    half = (slice(0, IH), slice(IH, 2 * IH))
    s_s = (s0_s, s1_s)
    e_s = (e0_s, e1_s)

    def position(b, parity):
        token = (b * 2 + parity) * bj
        token = (token // per + rows - row) % rows * per + token % per
        return pl.ds(pl.multiple_of(token, bj), bj)

    @pl.when(step == 0)
    def _():
        mask_s[...] = jnp.concatenate([mask_refs[r][...].astype(F32) for r in range(rows)], 1).T

        @pl.loop(0, blocks, unroll=4)
        def _(b):
            for src, par in ((mine_ref, core), (other_ref, 1 - core)):
                at = position(b, par)
                bias_s[at, :] = jnp.where(mask_s[at, 0:1] > 0, src[b].astype(F32) * LOG2E, NEG)
                acc_s[at, :] = jnp.zeros((bj, n_i), F32)

        e1_s[...] = jnp.zeros_like(e1_s)
        vt_s[...] = jnp.zeros_like(vt_s)
        g2_s[...] = jnp.zeros_like(g2_s)
        kc_s[...] = jnp.zeros_like(kc_s)

    tiles = range(0, n_j, JT)

    def scores(h):
        il = half[h]
        q = q_ref[0, :, il].astype(F32) * (scaling * LOG2E)
        qh = q.astype(BF16)
        ql = (q - qh.astype(F32)).astype(BF16)
        q2 = jnp.concatenate([qh, ql], 0)
        m = None
        for t in tiles:
            s = jnp.dot(kt_s[t:t + JT, :], q2, preferred_element_type=F32) + bias_s[t:t + JT, il]
            s_s[h][t:t + JT, :] = s
            mt = jnp.max(s.reshape(JT // 8, 8, IH), axis=0)
            m = mt if m is None else jnp.maximum(m, mt)
            yield None
        yield jnp.max(m, axis=0, keepdims=True)

    def soften(h, m):
        il = half[h]
        for t in tiles:
            e_s[h][t:t + JT, :] = jnp.exp2(s_s[h][t:t + JT, :] - m).astype(BF16)
            yield None
        v = jnp.concatenate([v_refs[r][...] for r in range(rows)], 1)
        o = jnp.dot(jnp.concatenate([v, jnp.ones((16, n_j), BF16)], 0), e_s[h][...], preferred_element_type=F32)
        yield None
        inv = 1.0 / o[dh:dh + 1, :]
        o = o[:dh] * inv
        o_ref[0, :, il] = o.astype(BF16)
        g = g_ref[0, :, il].astype(F32)
        centre = jnp.sum(g * o, axis=0, keepdims=True)
        g = g * inv
        c = -centre * inv
        gh = g.astype(BF16)
        gl = (g - gh.astype(F32)).astype(BF16)
        ch = c.astype(BF16).astype(F32)
        cl = c - ch
        line = lax.broadcasted_iota(jnp.int32, (16, IH), 0)
        cb = jnp.where(line == 0, ch, jnp.where(line == 1, cl, 0.0)).astype(BF16)
        yield jnp.concatenate([gh, gl, cb], 0)

    def backward(h, at, g2):
        il = half[h]
        dq = None
        for t in tiles:
            x = jnp.dot(vt_s[t:t + JT, :], g2, preferred_element_type=F32)
            ds = e_s[h][t:t + JT, :].astype(F32) * x
            acc_s[t:t + JT, il] += ds
            dt = jnp.dot(kc_s[:, t:t + JT], ds.astype(BF16), preferred_element_type=F32)
            dq = dt if dq is None else dq + dt
            yield None
        dq_ref[at, :, il] = (dq * scaling).astype(BF16)
        yield None

    def together(*chains):
        last = [None] * len(chains)
        live = list(range(len(chains)))
        while live:
            for n in list(live):
                try:
                    last[n] = next(chains[n])
                except StopIteration:
                    live.remove(n)
        return last

    for r in range(rows):
        sl = slice(r * per, (r + 1) * per)
        kz = k_refs[r][...] * mask_refs[r][0:1, :]
        kt_s[sl, :] = jnp.concatenate([kz, kz], 0).T
    m0, _ = together(scores(0), backward(1, jnp.maximum(step - 1, 0), g2_s[...]))
    for r in range(rows):
        sl = slice(r * per, (r + 1) * per)
        v = v_refs[r][...]
        vt_s[sl, :] = jnp.concatenate([v, v, jnp.ones((16, per), BF16)], 0).T
        kc_s[:, sl] = k_refs[r][...]
    g20, m1 = together(soften(0, m0), scores(1))
    _, g21 = together(backward(0, step, g20), soften(1, m1))
    g2_s[...] = g21

    @pl.when(step == steps - 1)
    def _():
        together(backward(1, step, g2_s[...]))

        @pl.loop(0, blocks, unroll=4)
        def _(b):
            for dst, par in ((keep_ref, core), (send_ref, 1 - core)):
                dst[b] = acc_s[position(b, par), :].astype(BF16)


def attention(place, mine, other, q, ks, vs, masks, g):
    S, dh, I = q.shape
    R, per = len(ks), ks[0].shape[1]
    J = R * per
    IH = I // 2
    full = lambda a: pl.BlockSpec(a.shape, lambda s: (0,) * a.ndim)
    one = pl.BlockSpec((1, dh, I), lambda s: (s, 0, 0))
    own = pl.BlockSpec((dh, per), lambda s: (s, 0))
    flags = pl.BlockSpec((MASK, per), lambda s: (0, 0))
    return pl.pallas_call(
        functools.partial(attend_kernel, R),
        grid=(S,),
        in_specs=[pl.BlockSpec(memory_space=pltpu.SMEM), full(mine), full(other), one, one]
        + [own] * (2 * R) + [flags] * R,
        out_specs=[one, full(q), full(mine), full(other)],
        out_shape=[jax.ShapeDtypeStruct(a.shape, BF16) for a in (q, q, mine, other)],
        scratch_shapes=[pltpu.VMEM((J, I), F32), pltpu.VMEM((J, I), F32),
                        pltpu.VMEM((J, IH), F32), pltpu.VMEM((J, IH), F32),
                        pltpu.VMEM((J, IH), BF16), pltpu.VMEM((J, IH), BF16),
                        pltpu.VMEM((J, 2 * dh), BF16), pltpu.VMEM((J, 2 * dh + 16), BF16),
                        pltpu.VMEM((dh, J), BF16), pltpu.VMEM((2 * dh + 16, IH), BF16),
                        pltpu.VMEM((J, 16), F32)],
        compiler_params=pltpu.CompilerParams(vmem_limit_bytes=121 * 512 * 1024),
        input_output_aliases={1: 2, 2: 3},
        cost_estimate=pl.CostEstimate(flops=8 * S * J * I * dh, bytes_accessed=12 << 20, transcendentals=S * I * J),
        name="attend",
    )(place, mine, other, q, g, *ks, *vs, *masks)


def weight_kernel(weight_ref, gain_ref, out_ref):
    scaled = weight_ref[...].astype(F32) * gain_ref[...]
    hi, lo = (x.astype(F32) for x in split(scaled - jnp.mean(scaled, axis=1, keepdims=True)))
    out_ref[...] = jnp.concatenate([spread(w) for w in (hi, hi, lo)], 0).T.astype(BF16)


def grad_weight(weight, gain):
    C, H = weight.shape
    return pl.pallas_call(
        weight_kernel,
        out_shape=jax.ShapeDtypeStruct((GROUP * C, 3 * H * GROUP), BF16),
        compiler_params=pltpu.CompilerParams(vmem_limit_bytes=32 * 1024 * 1024),
        name="grad_weight",
    )(weight.T, gain.reshape(1, C))


def local(pair, pair_gain, pair_weight, queries, keys, values, d_atoms, key_mask, atom_token):
    strip = queries.shape[3]
    swap = lambda x: lax.ppermute(x, "core", [(0, 1), (1, 0)])
    spread_out = lambda x: lax.all_to_all(x, ("col", "zhi"), 0, 0, tiled=True)

    rows = lax.axis_size("row")
    pass_on = lambda x, n: lax.ppermute(x, "row", [(i, (i + n) % rows) for i in range(rows)])
    k = keys.reshape(-1, strip)
    v = values.reshape(-1, strip)
    k_behind, v_ahead = pass_on(k, 1), pass_on(v, -1)
    bias = pair_bias(pair, pair_gain, pair_weight, lax.axis_size("zhi"))
    bias, k_later, v_later = lax.optimization_barrier((bias, k, v))
    k_ahead, v_behind = pass_on(k_later, -1), pass_on(v_later, 1)
    k_behind, v_ahead, again = lax.optimization_barrier((k_behind, v_ahead, pair))
    hat, inv = pair_hat(again)
    flags = jnp.broadcast_to(key_mask.astype(BF16), (MASK, strip))
    k_behind, v_ahead, hat, inv, flags = lax.optimization_barrier((k_behind, v_ahead, hat, inv, flags))
    ks = [k, k_ahead, pass_on(k_behind, 1), k_behind]
    vs = [v, v_ahead, pass_on(v_ahead, -1), v_behind]
    masks = [flags, pass_on(flags, -1), pass_on(flags, -2), pass_on(flags, 1)]
    place = jnp.stack([lax.axis_index("core"), lax.axis_index("row")]).astype(jnp.int32)

    heads, copies, width, _ = bias.shape
    mine = spread_out(bias.reshape(heads * copies, width, strip))

    offset = lax.axis_index("row") * strip
    onehot = (
        atom_token[:, None] - offset == jnp.arange(strip, dtype=jnp.int32)[None, :]
    ).astype(BF16)
    grad_out = jnp.einsum(
        "sda,at->sdt", d_atoms[:, 0], onehot, preferred_element_type=F32
    ).astype(BF16)
    weight = grad_weight(pair_weight, pair_gain)
    mine, ks, vs, masks, place, grad_out, weight, hat, inv = lax.optimization_barrier(
        (mine, ks, vs, masks, place, grad_out, weight, hat, inv))
    other = swap(mine)
    o, dq, keep, send = attention(place, mine, other, queries[:, 0], ks, vs, masks, grad_out)

    chip = (keep.astype(F32) + swap(send).astype(F32)).astype(BF16)
    d_pair = pair_grad(spread_out(chip), bias, inv, hat, weight)
    return (o[:, None], dq[:, None], d_pair)


def solution(mesh):
    fine = Mesh(mesh.devices.reshape(4, 16, 2, 2), ("row", "col", "zhi", "core"))
    sample = ("zhi", "core")
    tokens = P(sample, "col", None, "row")
    tile = P("row", ("col", "zhi", "core"), None)
    return jax.shard_map(
        local,
        mesh=fine,
        in_specs=(tile, P(), P(), tokens, tokens, tokens, tokens, P("row"), P("row")),
        out_specs=(tokens, tokens, tile),
        check_vma=False,
    )
```
